128 devices in a mesh: rep: 4 (over y), shard: 16 (over z, x_lo, core), tp: 2 (over x_hi).
Axes of the slice: x: 4 (x_hi: 2, x_lo: 2; x = x_hi * 2 + x_lo), y: 4, z: 4, core: 2. Of those that a mesh axis runs over, the one named last changes fastest.
Arguments:
- hidden_in: bfloat16 [32768, 8192], P(('rep', 'shard', 'tp')), may hold values from -6 to 6
- lengths: int32 [64], P(('rep', 'shard')), may hold values from 128 to 512, as said below
- kv_grad_out: bfloat16 [32768, 2, 1024], P(('rep', 'shard'), None, 'tp'), may hold values from -384 to 384
- master: float32 [8192, 2, 1024], P('shard', None, 'tp'), may hold values from -0.0625 to 0.0625
- moment_one: float32 [8192, 2, 1024], P('shard', None, 'tp'), may hold values from -3 to 3
- moment_two: float32 [8192, 2, 1024], P('shard', None, 'tp'), may hold values from 0.05 to 2
Outputs:
- new_master: float32 [8192, 2, 1024], P('shard', None, 'tp')
- new_moment_one: float32 [8192, 2, 1024], P('shard', None, 'tp')
- new_moment_two: float32 [8192, 2, 1024], P('shard', None, 'tp')
- fresh_kv: bfloat16 [32768, 2, 1024], P(('rep', 'shard'), None, 'tp')
The draws below stay inside these ranges and needn't reach their ends.
Inputs may be any that keep to these rules, and one draw needn't show every extreme that they name: In block b only its first lengths[b] tokens are valid.
All inputs are finite; a program needn't handle non-finite values.
Results may differ from the reference program's by a relative error of at most 0.014.
Values may be sent and summed in bfloat16 or wider, within the bound.
A program may use at most 192 MiB of HBM per device.

```python
import math
import jax
import jax.numpy as jnp
from jax import lax

D = 8192
KV = 1024
TOK_DEV = 512
BLOCKS = 64
TOKENS = 32768


def draw_lengths(key, part):
    key = jax.random.fold_in(key, 7)
    index = jnp.arange(BLOCKS, dtype=jnp.int32)
    base = TOK_DEV // 4 + 3 * TOK_DEV // 4 * index // max(BLOCKS - 1, 1)
    jitter = jax.random.randint(key, (BLOCKS,), 0, TOK_DEV // 8 + 1, dtype=jnp.int32)
    jitter = jnp.where(index == 0, 0, jitter)
    return jnp.minimum(base + jitter, TOK_DEV).astype(jnp.int32)


def steps_of(key, extent, shards, smallest, high):
    def one(dim, parts):
        draws = jax.random.uniform(jax.random.fold_in(jax.random.fold_in(key, 6), dim), (parts,), jnp.float32, smallest / len(shards), high / len(shards))
        return jnp.repeat(jnp.exp(draws), extent[dim] // parts).reshape((-1,) + (1,) * (len(extent) - dim - 1))

    loudness = one(*shards[0])
    for cut in shards[1:]:
        loudness = loudness * one(*cut)
    return loudness


def noise(rng, dims, width, limit, split=(), held_as=jnp.bfloat16):
    array = width * jax.random.normal(rng, dims, jnp.float32)
    if split:
        array = array * steps_of(rng, dims, split, -0.22, 0.18)
    return jnp.clip(array, -limit, limit).astype(held_as)


def setup_inputs(seed: int = 0) -> dict:
    splits = jax.random.split(jax.random.key(seed), 7)
    hidden_in = noise(splits[0], (TOKENS, D), 1.0, 6.0, ((0, 128),))
    lengths = draw_lengths(jax.random.fold_in(splits[6], 71), 0)
    kv_grad_out = noise(splits[2], (TOKENS, 2, KV), 64.0, 384.0, ((0, 64), (2, 2)))
    master = noise(splits[3], (D, 2, KV), D ** -0.5, 0.0625, ((0, 16), (2, 2)), jnp.float32)
    moment_one = noise(splits[4], (D, 2, KV), 0.5, 3.0, ((0, 16), (2, 2)), jnp.float32)
    moment_two = jnp.clip(jnp.exp(math.log(2.0) - 3.6888794 * jax.random.uniform(splits[5], (D, 2, KV), jnp.float32) ** steps_of(splits[5], (D, 2, KV), ((0, 16), (2, 2)), -0.2, 0.2)), 0.05, 2.0)
    return dict(hidden_in=hidden_in, lengths=lengths, kv_grad_out=kv_grad_out, master=master, moment_one=moment_one, moment_two=moment_two)


beta_one = 0.9
beta_two = 0.95
step_count = 20
rate = 0.002
decay = 0.1
epsilon = 1e-08

def adamw(master, moment_one, moment_two, grad):
    first = beta_one * moment_one + (1.0 - beta_one) * grad
    second = beta_two * moment_two + (1.0 - beta_two) * grad * grad
    first_hat = first / (1.0 - beta_one ** step_count)
    second_hat = second / (1.0 - beta_two ** step_count)
    updated = master - rate * (first_hat / (jnp.sqrt(second_hat) + epsilon) + decay * master)
    return (updated, first, second)

def reference(hidden_in, lengths, kv_grad_out, master, moment_one, moment_two):
    count = jnp.sum(lengths.astype(jnp.float32))
    flat_cot = kv_grad_out.reshape(TOKENS, 2 * KV)

    def accumulate(total, block):
        start = block * TOK_DEV
        inputs = lax.dynamic_slice_in_dim(hidden_in, start, TOK_DEV, 0)
        cotan = lax.dynamic_slice_in_dim(flat_cot, start, TOK_DEV, 0)
        validity = (jnp.arange(TOK_DEV, dtype=jnp.int32) < lengths[block]).astype(cotan.dtype)
        cotan = cotan * validity[:, None]
        term = lax.dot_general(inputs, cotan, (((0,), (0,)), ((), ())), preferred_element_type=jnp.float32)
        rounded = lax.optimization_barrier(term.astype(jnp.bfloat16))
        return (total + rounded.astype(jnp.float32), None)
    summed, _ = lax.scan(accumulate, jnp.zeros((D, 2 * KV), jnp.float32), jnp.arange(BLOCKS, dtype=jnp.int32))
    grad = summed.reshape(D, 2, KV) / count
    new_master, new_first, new_second = adamw(master, moment_one, moment_two, grad)
    weights = new_master.astype(jnp.bfloat16).reshape(D, 2 * KV)

    def project(block):
        inputs = lax.dynamic_slice_in_dim(hidden_in, block * TOK_DEV, TOK_DEV, 0)
        return jnp.dot(inputs, weights, preferred_element_type=jnp.float32).astype(jnp.bfloat16)
    fresh = lax.map(project, jnp.arange(BLOCKS, dtype=jnp.int32))
    return (new_master, new_first, new_second, fresh.reshape(TOKENS, 2, KV))
```

```python
import functools

import jax
import jax.numpy as jnp
from jax import lax
from jax.experimental import pallas as pl
from jax.experimental.pallas import tpu as pltpu
from jax.sharding import PartitionSpec as P

MESH = pl.DeviceIdType.MESH
F32, BF16 = jnp.float32, jnp.bfloat16

beta_one = 0.9
beta_two = 0.95
step_count = 20
rate = 0.002
decay = 0.1
epsilon = 1e-08

NJ = 4
TOK = 512
FEAT = 1024
HALF = 512


def adamw(master, moment_one, moment_two, grad):
    first = beta_one * moment_one + (1.0 - beta_one) * grad
    second = beta_two * moment_two + (1.0 - beta_two) * grad * grad
    first_hat = first / (1.0 - beta_one**step_count)
    second_hat = second / (1.0 - beta_two**step_count)
    updated = master - rate * (first_hat / (jnp.sqrt(second_hat) + epsilon) + decay * master)
    return (updated, first, second)


def main_kernel(
    hid,
    lengths,
    kv,
    master,
    first,
    second,
    fresh_out,
    g_out,
    count_out,
    hbuf,
    cbuf,
    kvbuf,
    gbuf,
    r1,
    r2a,
    r2b,
    r3,
    r4,
    wbuf,
    acc,
    fsend,
    frecv,
    mbuf,
    cnt,
    send_s,
    recv_s,
    gg_s,
    gg_r,
    h_s,
    h_r,
    h_l,
    small_s,
    small_r,
    load_s,
):
    y = lax.axis_index("rep")
    s = lax.axis_index("shard")
    t = lax.axis_index("tp")
    z = s // 4
    xl = (s // 2) % 2
    c = s % 2

    def ydev(d):
        return ((y + d) % 4, s, t)

    def zdev(d):
        return (y, ((z + d) % 4) * 4 + s % 4, t)

    xdev = (y, z * 4 + (1 - xl) * 2 + c, t)
    sib = (y, z * 4 + xl * 2 + (1 - c), t)

    def partner(core):
        return (y, z * 4 + xl * 2 + core, 1 - t)

    peers = [ydev(1), ydev(2), ydev(3), zdev(1), zdev(2), zdev(3), xdev, sib, partner(0), partner(1)]
    sends = []

    def put(src, dst, ss, rs, dev):
        copy = pltpu.make_async_remote_copy(src, dst, ss, rs, device_id=dev, device_id_type=MESH)
        copy.start()
        sends.append(copy)

    def got(dst, rs):
        pltpu.make_async_remote_copy(dst, dst, rs, rs, device_id=sib, device_id_type=MESH).wait_recv()

    kv_load = pltpu.make_async_copy(kv, kvbuf, load_s.at[3])
    kv_load.start()
    loads = []
    for k, ref in enumerate((master, first, second)):
        for j in range(NJ):
            loads.append(
                pltpu.make_async_copy(
                    ref.at[pl.ds(j * 128 + y * 32, 32)], mbuf.at[k, j], load_s.at[4 + k * NJ + j]
                )
            )
    for load in loads:
        load.start()

    mine = pl.ds(pl.multiple_of(c * 512 + t * 256, 256), 256)

    def columns(j, q, core):
        return pl.ds(pl.multiple_of((2 * q + core) * 512 + j * 128, 128), 128)

    def h_local(j):
        @pl.loop(0, 8)
        def _(q):
            pltpu.make_async_copy(
                hid.at[:, columns(j, q, c)],
                hbuf.at[j, mine, pl.ds(pl.multiple_of(q * 128, 128), 128)],
                h_l.at[j],
            ).start()

    def h_send(j):
        for k, (dev, core) in enumerate(((partner(0), 0), (partner(1), 1), (sib, 1 - c))):

            @pl.loop(0, 8)
            def _(q):
                pltpu.make_async_remote_copy(
                    hid.at[:, columns(j, q, core)],
                    hbuf.at[j, mine, pl.ds(pl.multiple_of(q * 128, 128), 128)],
                    h_s.at[j, k],
                    h_r.at[j, c * 2 + t],
                    device_id=dev,
                    device_id_type=MESH,
                ).start()

    def h_wait(j):
        pltpu.make_async_copy(hbuf.at[j, mine], hbuf.at[j, mine], h_l.at[j]).wait()
        for core, tp in ((1 - c, t), (0, 1 - t), (1, 1 - t)):
            rows = pl.ds(pl.multiple_of(core * 512 + tp * 256, 256), 256)
            got(hbuf.at[j, rows], h_r.at[j, core * 2 + tp])

    for j in range(NJ):
        h_local(j)

    barrier = pltpu.get_barrier_semaphore()
    for dev in peers:
        pl.semaphore_signal(barrier, inc=1, device_id=dev, device_id_type=MESH)
    pl.semaphore_wait(barrier, len(peers))

    h_send(0)
    h_send(1)

    def count_step(base, n, me, devs, sem):
        for d in range(1, n):
            put(cnt.at[base + me], cnt.at[base + me], small_s.at[sem + d], small_r.at[sem + d], devs(d))

    def count_sum(base, n, me, sem):
        for d in range(1, n):
            got(cnt.at[base + (me + n - d) % n], small_r.at[sem + d])
        total = cnt[base]
        for d in range(1, n):
            total = total + cnt[base + d]
        return total

    cnt[y] = jnp.full((8, 128), lengths[0], jnp.int32).astype(F32)
    count_step(0, 4, y, ydev, 0)

    kv_load.wait()

    @pl.loop(0, 8)
    def _(b):
        rows = pl.ds(pl.multiple_of(b * 64, 64), 64)
        value = kvbuf[rows].astype(F32)
        token = lax.broadcasted_iota(jnp.int32, (64, 8, 128), 0) + b * 64
        value = jnp.where(token < lengths[0], value, 0.0)
        cbuf[pl.ds(pl.multiple_of(c * 512 + b * 64, 64), 64)] = value.reshape(64, FEAT).astype(BF16)

    own_c = cbuf.at[pl.ds(pl.multiple_of(c * 512, 512), 512)]
    sib_c = cbuf.at[pl.ds(pl.multiple_of((1 - c) * 512, 512), 512)]
    put(own_c, own_c, small_s.at[0], small_r.at[0], sib)

    cnt[4 + z] = count_sum(0, 4, y, 0)
    count_step(4, 4, z, zdev, 4)
    cnt[8 + xl] = count_sum(4, 4, z, 4)
    count_step(8, 2, xl, lambda d: xdev, 8)
    cnt[10 + c] = count_sum(8, 2, xl, 8)
    count_step(10, 2, c, lambda d: sib, 10)
    count_out[...] = count_sum(10, 2, c, 10)

    got(sib_c, small_r.at[0])

    index = ((y, z), (z, y))
    devs = ((ydev, zdev), (zdev, ydev))
    r2 = (r2a, r2b)
    every = slice(None)

    def at(h, a1, a2, x=every):
        if h == 0:
            return (a2, x, a1)
        return (a1, x, a2)

    def unit(buf, j, h, a1, a2=every, x=every):
        return buf.at[(j, h) + at(h, a1, a2, x)]

    LOW, HIGH = pl.ds(0, 2), pl.ds(2, 2)

    def g0(j):
        h_wait(j)
        if j + 2 < NJ:
            h_send(j + 2)

        @pl.loop(0, 4)
        def _(zz):
            left = hbuf[j, :, pl.ds(pl.multiple_of(zz * 256, 256), 256)]
            for h in range(2):
                part = lax.dot_general(
                    left,
                    cbuf[:, h * HALF : (h + 1) * HALF],
                    (((0,), (0,)), ((), ())),
                    preferred_element_type=F32,
                )
                gbuf[j, h, zz] = part.astype(BF16).reshape(2, 4, 32, HALF)

        for h in range(2):
            i1 = index[h][0]
            far = (i1 + 2) % 4
            put(unit(gbuf, j, h, far, LOW), r1.at[j, h, 0], send_s.at[j, h, 0], recv_s.at[j, h, 0], devs[h][0](1))
            put(unit(gbuf, j, h, far, HIGH), r1.at[j, h, 1], send_s.at[j, h, 1], recv_s.at[j, h, 1], devs[h][0](3))

    def g1(j):
        for h in range(2):
            i1 = index[h][0]
            for k, (d, low) in enumerate(((1, 0), (3, 2))):
                got(r1.at[j, h, k], recv_s.at[j, h, k])
                to = (i1 + d) % 4
                for a in range(2):
                    for b in range(2):
                        if h == 0:
                            spot = (j, h, low + a, b, to)
                        else:
                            spot = (j, h, to, a, low + b)
                        gbuf[spot] = (gbuf[spot].astype(F32) + r1[j, h, k, a, b].astype(F32)).astype(BF16)
                put(unit(gbuf, j, h, to), r2[h].at[j, k], send_s.at[j, h, 2 + k], recv_s.at[j, h, 2 + k], devs[h][0](d))

    def g2(j):
        for h in range(2):
            i1, i2 = index[h]
            for k in range(2):
                got(r2[h].at[j, k], recv_s.at[j, h, 2 + k])

            @pl.loop(0, 8)
            def _(n):
                a2, x = n // 2, n % 2
                spot = (j, h) + at(h, i1, a2, x)
                here = (a2, x) if h == 0 else (x, a2)
                gbuf[spot] = (
                    gbuf[spot].astype(F32)
                    + r2[h][(j, 0) + here].astype(F32)
                    + r2[h][(j, 1) + here].astype(F32)
                ).astype(BF16)

            for d in range(1, 4):
                put(
                    unit(gbuf, j, h, i1, (i2 + d) % 4),
                    r3.at[j, h, d - 1],
                    send_s.at[j, h, 3 + d],
                    recv_s.at[j, h, 3 + d],
                    devs[h][1](d),
                )

    def g3(j):
        for h in range(2):
            i1, i2 = index[h]
            for d in range(1, 4):
                got(r3.at[j, h, d - 1], recv_s.at[j, h, 3 + d])
            for x in range(2):
                spot = (j, h) + at(h, i1, i2, x)
                total = gbuf[spot].astype(F32)
                for d in range(3):
                    total = total + r3[j, h, d, x].astype(F32)
                gbuf[spot] = total.astype(BF16)
            put(unit(gbuf, j, h, i1, i2, 1 - xl), r4.at[j, h], send_s.at[j, h, 7], recv_s.at[j, h, 7], xdev)

    def g4(j):
        for k in range(3):
            loads[k * NJ + j].wait()
        count = jnp.broadcast_to(count_out[0:1, 0:1], (32, FEAT))
        halves = []
        for h in range(2):
            i1, i2 = index[h]
            got(r4.at[j, h], recv_s.at[j, h, 7])
            halves.append(gbuf[(j, h) + at(h, i1, i2, xl)].astype(F32) + r4[j, h].astype(F32))
        summed = jnp.concatenate(halves, axis=1).astype(BF16)
        g_out[j, y] = summed
        grad = summed.astype(F32) / count
        new, _, _ = adamw(
            mbuf[0, j].reshape(32, FEAT), mbuf[1, j].reshape(32, FEAT), mbuf[2, j].reshape(32, FEAT), grad
        )
        new = new.astype(BF16)
        for h in range(2):
            i1, i2 = index[h]
            wbuf[(j, h) + at(h, i1, i2, xl)] = new[:, h * HALF : (h + 1) * HALF]
            own = unit(wbuf, j, h, i1, i2, xl)
            put(own, own, send_s.at[j, h, 8], recv_s.at[j, h, 8], xdev)
        for d in range(1, 4):
            put(g_out.at[j, y], g_out.at[j, y], gg_s.at[j, d - 1], gg_r.at[j, d - 1], ydev(d))

    def w1(j):
        for h in range(2):
            i1, i2 = index[h]
            got(unit(wbuf, j, h, i1, i2, 1 - xl), recv_s.at[j, h, 8])
            for d in range(1, 4):
                own = unit(wbuf, j, h, i1, i2)
                put(own, own, send_s.at[j, h, 8 + d], recv_s.at[j, h, 8 + d], devs[h][1](d))

    def w2(j):
        for h in range(2):
            i1, i2 = index[h]
            for d in range(1, 4):
                got(unit(wbuf, j, h, i1, (i2 + 4 - d) % 4), recv_s.at[j, h, 8 + d])
            own = unit(wbuf, j, h, i1)
            for k, d in enumerate((1, 3)):
                put(own, own, send_s.at[j, h, 12 + k], recv_s.at[j, h, 12 + k], devs[h][0](d))

    def w3(j):
        for h in range(2):
            i1 = index[h][0]
            for k, (d, part) in enumerate(((1, LOW), (3, HIGH))):
                back = (i1 + 4 - d) % 4
                got(unit(wbuf, j, h, back), recv_s.at[j, h, 12 + k])
                piece = unit(wbuf, j, h, back, part)
                put(piece, piece, send_s.at[j, h, 14 + k], recv_s.at[j, h, 14 + k], devs[h][0](d))

    def w4(j):
        for h in range(2):
            far = (index[h][0] + 2) % 4
            for k, part in enumerate((LOW, HIGH)):
                got(unit(wbuf, j, h, far, part), recv_s.at[j, h, 14 + k])
        if j < NJ - 1:

            @pl.loop(0, 4)
            def _(b):
                rows = pl.ds(pl.multiple_of(b * 256, 256), 256)
                left = hbuf[j, rows]
                for h in range(2):
                    part = jnp.dot(left, wbuf[j, h].reshape(1024, HALF), preferred_element_type=F32)
                    cols = slice(h * HALF, (h + 1) * HALF)
                    if j == 0:
                        acc[rows, cols] = part
                    else:
                        acc[rows, cols] += part
        else:
            for own in range(2):
                core = c if own else 1 - c

                @pl.loop(0, 2)
                def _(b):
                    rows = pl.ds(pl.multiple_of(core * 512 + b * 256, 256), 256)
                    here = pl.ds(pl.multiple_of(b * 256, 256), 256)
                    left = hbuf[j, rows]
                    for h in range(2):
                        part = jnp.dot(left, wbuf[j, h].reshape(1024, HALF), preferred_element_type=F32)
                        cols = slice(h * HALF, (h + 1) * HALF)
                        if own:
                            acc[rows, cols] += part
                        else:
                            fsend[here, cols] = (acc[rows, cols] + part).astype(BF16)

                if not own:
                    put(fsend, frecv, small_s.at[12], small_r.at[12], sib)
            got(frecv, small_r.at[12])

            @pl.loop(0, 4)
            def _(b):
                rows = pl.ds(pl.multiple_of(c * 512 + b * 128, 128), 128)
                here = pl.ds(pl.multiple_of(b * 128, 128), 128)
                fresh_out[here] = (acc[rows] + frecv[here].astype(F32)).astype(BF16)

    g0(0)
    g1(0)
    g2(0)
    g3(0)
    g4(0)
    for j in range(1, NJ):
        w1(j - 1)
        g0(j)
        w2(j - 1)
        g1(j)
        w3(j - 1)
        g2(j)
        w4(j - 1)
        g3(j)
        g4(j)
    w1(NJ - 1)
    w2(NJ - 1)
    w3(NJ - 1)
    w4(NJ - 1)

    for j in range(NJ):
        for d in range(1, 4):
            got(g_out.at[j, (y + 4 - d) % 4], gg_r.at[j, d - 1])
        for k in range(3):
            whole = hbuf.at[j, mine]
            pltpu.make_async_remote_copy(
                whole, whole, h_s.at[j, k], h_s.at[j, k], device_id=sib, device_id_type=MESH
            ).wait_send()
    for copy in sends:
        copy.wait_send()


def finish_kernel(g, count, master, first, second, fresh, new_master, new_first, new_second, fresh_out):
    rows = master.shape[0]
    summed = g[...].astype(F32).reshape(rows, 8, 128)
    grad = summed / jnp.broadcast_to(count[...][0:1, 0:1].reshape(1, 1, 1), (rows, 8, 128))
    a, b, d = adamw(master[...], first[...], second[...], grad)
    new_master[...] = a
    new_first[...] = b
    new_second[...] = d
    fresh_out[...] = fresh[...].astype(F32).reshape(rows, 8, 128).astype(BF16)


def tiles(array):
    n = array.shape[0]
    return array.reshape(n, 2, 4, 128).transpose(0, 2, 1, 3).reshape(n, 8, 128)


def untiles(array):
    n = array.shape[0]
    return array.reshape(n, 4, 2, 128).transpose(0, 2, 1, 3).reshape(n, 2, 512)


def local(hidden_in, lengths, kv_grad_out, master, moment_one, moment_two):
    kv = tiles(kv_grad_out)
    states = [tiles(a) for a in (master, moment_one, moment_two)]
    hbm = pl.BlockSpec(memory_space=pl.ANY)
    vmem = pl.BlockSpec(memory_space=pltpu.VMEM)
    dma = pltpu.SemaphoreType.DMA
    fresh, g, count = pl.pallas_call(
        main_kernel,
        out_shape=(
            jax.ShapeDtypeStruct((TOK, FEAT), BF16),
            jax.ShapeDtypeStruct((NJ, 4, 32, FEAT), BF16),
            jax.ShapeDtypeStruct((8, 128), F32),
        ),
        in_specs=[hbm, pl.BlockSpec(memory_space=pltpu.SMEM), hbm, hbm, hbm, hbm],
        out_specs=(vmem, vmem, vmem),
        scratch_shapes=[
            pltpu.VMEM((NJ, 1024, 1024), BF16),
            pltpu.VMEM((1024, FEAT), BF16),
            pltpu.VMEM((TOK, 8, 128), BF16),
            pltpu.VMEM((NJ, 2, 4, 2, 4, 32, HALF), BF16),
            pltpu.VMEM((NJ, 2, 2, 2, 2, 32, HALF), BF16),
            pltpu.VMEM((NJ, 2, 4, 2, 32, HALF), BF16),
            pltpu.VMEM((NJ, 2, 2, 4, 32, HALF), BF16),
            pltpu.VMEM((NJ, 2, 3, 2, 32, HALF), BF16),
            pltpu.VMEM((NJ, 2, 32, HALF), BF16),
            pltpu.VMEM((NJ, 2, 4, 2, 4, 32, HALF), BF16),
            pltpu.VMEM((1024, FEAT), F32),
            pltpu.VMEM((TOK, FEAT), BF16),
            pltpu.VMEM((TOK, FEAT), BF16),
            pltpu.VMEM((3, NJ, 32, 8, 128), F32),
            pltpu.VMEM((12, 8, 128), F32),
            dma((NJ, 2, 16)),
            dma((NJ, 2, 16)),
            dma((NJ, 3)),
            dma((NJ, 3)),
            dma((NJ, 3)),
            dma((NJ, 4)),
            dma((NJ,)),
            dma((13,)),
            dma((13,)),
            dma((4 + 3 * NJ,)),
        ],
        compiler_params=pltpu.CompilerParams(
            collective_id=0, has_side_effects=True, vmem_limit_bytes=60 * 2**20
        ),
        name="project",
    )(hidden_in, lengths, kv, *states)
    g = g.reshape(TOK, FEAT)
    step = 64
    flat = pl.BlockSpec((step, FEAT), lambda i: (i, 0))
    cube = pl.BlockSpec((step, 8, 128), lambda i: (i, 0, 0))
    outs = pl.pallas_call(
        finish_kernel,
        grid=(TOK // step,),
        out_shape=[jax.ShapeDtypeStruct((TOK, 8, 128), F32)] * 3
        + [jax.ShapeDtypeStruct((TOK, 8, 128), BF16)],
        in_specs=[flat, pl.BlockSpec((8, 128), lambda i: (0, 0)), cube, cube, cube, flat],
        out_specs=[cube] * 4,
        compiler_params=pltpu.CompilerParams(vmem_limit_bytes=32 * 2**20),
        name="update",
    )(g, count, *states, fresh)
    return tuple(untiles(a) for a in outs)


def solution(mesh):
    in_specs = (
        P(("rep", "shard", "tp"), None),
        P(("rep", "shard")),
        P(("rep", "shard"), None, "tp"),
        P("shard", None, "tp"),
        P("shard", None, "tp"),
        P("shard", None, "tp"),
    )
    out_specs = (
        P("shard", None, "tp"),
        P("shard", None, "tp"),
        P("shard", None, "tp"),
        P(("rep", "shard"), None, "tp"),
    )
    return jax.shard_map(local, mesh=mesh, in_specs=in_specs, out_specs=out_specs, check_vma=False)
```

```python
import functools

import jax
import jax.numpy as jnp
from jax import lax
from jax.experimental import pallas as pl
from jax.experimental.pallas import tpu as pltpu
from jax.sharding import PartitionSpec as P

MESH = pl.DeviceIdType.MESH
F32, BF16 = jnp.float32, jnp.bfloat16

beta_one = 0.9
beta_two = 0.95
step_count = 20
rate = 0.002
decay = 0.1
epsilon = 1e-08

NJ = 4
TOK = 512
FEAT = 1024
HALF = 512


def schedule():
    order = []

    def add(stage, j, x=0):
        if 0 <= j < NJ:
            order.append((stage, j, x))

    for i in range(NJ + 1):
        add("g2", i - 1, 1)
        add("g0", i, 0)
        add("wc", i - 2, 1)
        add("g3", i - 1, 1)
        add("gx", i - 1)
        add("g1", i, 0)
        add("wd", i - 2, 0)
        add("wd", i - 2, 1)
        add("gy", i - 1)
        add("g2", i, 0)
        add("g0", i, 1)
        add("wa", i - 1, 1)
        add("wb", i - 1, 0)
        add("g1", i, 1)
        add("wb", i - 1, 1)
        add("g3", i, 0)
        add("wc", i - 1, 0)
        add("gg", i - 1)
    j = NJ - 1
    return order + [("wc", j, 1), ("wd", j, 0), ("wd", j, 1), ("last", 0, 0)]


def adamw(master, moment_one, moment_two, grad):
    first = beta_one * moment_one + (1.0 - beta_one) * grad
    second = beta_two * moment_two + (1.0 - beta_two) * grad * grad
    first_hat = first / (1.0 - beta_one**step_count)
    second_hat = second / (1.0 - beta_two**step_count)
    updated = master - rate * (first_hat / (jnp.sqrt(second_hat) + epsilon) + decay * master)
    return (updated, first, second)


def main_kernel(
    hid,
    lengths,
    kv,
    master,
    first,
    second,
    fresh_out,
    g_out,
    count_out,
    hbuf,
    cbuf,
    kvbuf,
    gbuf,
    r1,
    r2,
    r3,
    r4,
    wbuf,
    acc,
    fsend,
    frecv,
    mbuf,
    cnt,
    send_s,
    recv_s,
    gg_s,
    gg_r,
    h_s,
    h_r,
    h_l,
    small_s,
    small_r,
    load_s,
):
    y = lax.axis_index("rep")
    s = lax.axis_index("shard")
    t = lax.axis_index("tp")
    z = s // 4
    xl = (s // 2) % 2
    c = s % 2

    def ydev(d):
        return ((y + d) % 4, s, t)

    def zdev(d):
        return (y, ((z + d) % 4) * 4 + s % 4, t)

    xdev = (y, z * 4 + (1 - xl) * 2 + c, t)
    sib = (y, z * 4 + xl * 2 + (1 - c), t)

    def partner(core):
        return (y, z * 4 + xl * 2 + core, 1 - t)

    peers = [ydev(1), ydev(2), ydev(3), zdev(1), zdev(2), zdev(3), xdev, sib, partner(0), partner(1)]
    sends = []

    def put(src, dst, ss, rs, dev):
        copy = pltpu.make_async_remote_copy(src, dst, ss, rs, device_id=dev, device_id_type=MESH)
        copy.start()
        sends.append(copy)

    def got(dst, rs):
        pltpu.make_async_remote_copy(dst, dst, rs, rs, device_id=sib, device_id_type=MESH).wait_recv()

    mine = pl.ds(pl.multiple_of(c * 512 + t * 256, 256), 256)

    def columns(j, x, n, core):
        return pl.ds(pl.multiple_of((4 * n + 2 * x + core) * 512 + j * 128, 128), 128)

    def lanes(n):
        return pl.ds(pl.multiple_of(n * 128, 128), 128)

    def h_local(j, x):
        @pl.loop(0, 4)
        def _(n):
            pltpu.make_async_copy(
                hid.at[:, columns(j, x, n, c)], hbuf.at[j, x, mine, lanes(n)], h_l.at[j, x]
            ).start()

    def h_send(j, x):
        for k, (dev, core) in enumerate(((partner(0), 0), (partner(1), 1), (sib, 1 - c))):

            @pl.loop(0, 4)
            def _(n):
                pltpu.make_async_remote_copy(
                    hid.at[:, columns(j, x, n, core)],
                    hbuf.at[j, x, mine, lanes(n)],
                    h_s.at[j, x, k],
                    h_r.at[j, x, c * 2 + t],
                    device_id=dev,
                    device_id_type=MESH,
                ).start()

    def h_wait(j, x):
        pltpu.make_async_copy(hbuf.at[j, x, mine], hbuf.at[j, x, mine], h_l.at[j, x]).wait()
        for core, tp in ((1 - c, t), (0, 1 - t), (1, 1 - t)):
            rows = pl.ds(pl.multiple_of(core * 512 + tp * 256, 256), 256)
            got(hbuf.at[j, x, rows], h_r.at[j, x, core * 2 + tp])

    barrier = pltpu.get_barrier_semaphore()
    for dev in peers:
        pl.semaphore_signal(barrier, inc=1, device_id=dev, device_id_type=MESH)
    pl.semaphore_wait(barrier, len(peers))

    h_send(0, 0)

    kv_load = pltpu.make_async_copy(kv, kvbuf, load_s.at[3])
    kv_load.start()
    for m in range(2 * NJ):
        h_local(m // 2, m % 2)
    loads = []
    for k, ref in enumerate((master, first, second)):
        for j in range(NJ):
            loads.append(
                pltpu.make_async_copy(
                    ref.at[pl.ds(j * 128 + y * 32, 32)], mbuf.at[k, j], load_s.at[4 + k * NJ + j]
                )
            )
    for load in loads:
        load.start()

    def count_step(base, n, me, devs, sem):
        for d in range(1, n):
            put(cnt.at[base + me], cnt.at[base + me], small_s.at[sem + d], small_r.at[sem + d], devs(d))

    def count_sum(base, n, me, sem):
        for d in range(1, n):
            got(cnt.at[base + (me + n - d) % n], small_r.at[sem + d])
        total = cnt[base]
        for d in range(1, n):
            total = total + cnt[base + d]
        return total

    cnt[y] = jnp.full((8, 128), lengths[0], jnp.int32).astype(F32)
    count_step(0, 4, y, ydev, 0)

    kv_load.wait()

    @pl.loop(0, 8)
    def _(b):
        rows = pl.ds(pl.multiple_of(b * 64, 64), 64)
        value = kvbuf[rows].astype(F32)
        token = lax.broadcasted_iota(jnp.int32, (64, 8, 128), 0) + b * 64
        value = jnp.where(token < lengths[0], value, 0.0)
        cbuf[pl.ds(pl.multiple_of(c * 512 + b * 64, 64), 64)] = value.reshape(64, FEAT).astype(BF16)

    own_c = cbuf.at[pl.ds(pl.multiple_of(c * 512, 512), 512)]
    sib_c = cbuf.at[pl.ds(pl.multiple_of((1 - c) * 512, 512), 512)]
    put(own_c, own_c, small_s.at[0], small_r.at[0], sib)

    cnt[4 + z] = count_sum(0, 4, y, 0)
    count_step(4, 4, z, zdev, 4)
    cnt[8 + xl] = count_sum(4, 4, z, 4)
    count_step(8, 2, xl, lambda d: xdev, 8)
    cnt[10 + c] = count_sum(8, 2, xl, 8)
    count_step(10, 2, c, lambda d: sib, 10)
    count_out[...] = count_sum(10, 2, c, 10)

    got(sib_c, small_r.at[0])

    index = ((y, z), (z, y))
    devs = ((ydev, zdev), (zdev, ydev))
    every = slice(None)
    LOW, HIGH = pl.ds(0, 2), pl.ds(2, 2)

    def at(j, x, h, a1, a2=every):
        return (j, x, h, a2, a1) if h == 0 else (j, x, h, a1, a2)

    def g0(j, x):
        h_wait(j, x)
        m = 2 * j + x
        for ahead in (m + 1,):
            if ahead < 2 * NJ:
                h_send(ahead // 2, ahead % 2)

        @pl.loop(0, 2)
        def _(n):
            left = hbuf[j, x, :, pl.ds(pl.multiple_of(n * 256, 256), 256)]
            pair = pl.ds(n * 2, 2)
            for h in range(2):
                part = lax.dot_general(
                    left,
                    cbuf[:, h * HALF : (h + 1) * HALF],
                    (((0,), (0,)), ((), ())),
                    preferred_element_type=F32,
                )
                gbuf[j, x, h, pair] = part.astype(BF16).reshape(2, 4, 32, HALF)

        for h in range(2):
            far = (index[h][0] + 2) % 4
            for k, (d, part) in enumerate(((1, LOW), (3, HIGH))):
                put(
                    gbuf.at[at(j, x, h, far, part)],
                    r1.at[j, x, h, k],
                    send_s.at[j, x, h, k],
                    recv_s.at[j, x, h, k],
                    devs[h][0](d),
                )

    def g1(j, x):
        for h in range(2):
            i1 = index[h][0]
            for k, (d, low) in enumerate(((1, 0), (3, 2))):
                got(r1.at[j, x, h, k], recv_s.at[j, x, h, k])
                to = (i1 + d) % 4
                for a in range(2):
                    spot = at(j, x, h, to, low + a)
                    gbuf[spot] = (gbuf[spot].astype(F32) + r1[j, x, h, k, a].astype(F32)).astype(BF16)
                put(
                    gbuf.at[at(j, x, h, to)],
                    r2.at[j, x, h, k],
                    send_s.at[j, x, h, 2 + k],
                    recv_s.at[j, x, h, 2 + k],
                    devs[h][0](d),
                )

    def g2(j, x):
        for h in range(2):
            i1, i2 = index[h]
            for k in range(2):
                got(r2.at[j, x, h, k], recv_s.at[j, x, h, 2 + k])
            for d in (2, 1, 3, 0):
                a2 = (i2 + d) % 4
                spot = at(j, x, h, i1, a2)
                gbuf[spot] = (
                    gbuf[spot].astype(F32) + r2[j, x, h, 0, a2].astype(F32) + r2[j, x, h, 1, a2].astype(F32)
                ).astype(BF16)
                if d:
                    put(
                        gbuf.at[spot],
                        r3.at[j, x, h, d - 1],
                        send_s.at[j, x, h, 3 + d],
                        recv_s.at[j, x, h, 3 + d],
                        devs[h][1](d),
                    )

    def g3(j, x):
        for h in range(2):
            i1, i2 = index[h]
            for d in range(1, 4):
                got(r3.at[j, x, h, d - 1], recv_s.at[j, x, h, 3 + d])
            spot = at(j, x, h, i1, i2)
            total = gbuf[spot].astype(F32)
            for d in range(3):
                total = total + r3[j, x, h, d].astype(F32)
            gbuf[spot] = total.astype(BF16)

    def gx(j):
        for h in range(2):
            put(gbuf.at[at(j, 1 - xl, h, *index[h])], r4.at[j, h], send_s.at[j, 0, h, 14], recv_s.at[j, 0, h, 14], xdev)

    def gy(j):
        for k in range(3):
            loads[k * NJ + j].wait()
        count = jnp.broadcast_to(count_out[0:1, 0:1], (32, FEAT))
        halves = []
        for h in range(2):
            got(r4.at[j, h], recv_s.at[j, 0, h, 14])
            halves.append(gbuf[at(j, xl, h, *index[h])].astype(F32) + r4[j, h].astype(F32))
        summed = jnp.concatenate(halves, axis=1).astype(BF16)
        g_out[j, y] = summed
        grad = summed.astype(F32) / count
        new, _, _ = adamw(*(mbuf[k, j].reshape(32, FEAT) for k in range(3)), grad)
        new = new.astype(BF16)
        for h in range(2):
            spot = at(j, xl, h, *index[h])
            wbuf[spot] = new[:, h * HALF : (h + 1) * HALF]
            own = wbuf.at[spot]
            put(own, own, send_s.at[j, 0, h, 15], recv_s.at[j, 0, h, 15], xdev)
        wa(j, 0)

    def gg(j):
        for d in range(1, 4):
            put(g_out.at[j, y], g_out.at[j, y], gg_s.at[j, d - 1], gg_r.at[j, d - 1], ydev(d))

    def side(k):
        return 1 - xl if k else xl

    def wa(j, k):
        for h in range(2):
            own = wbuf.at[at(j, side(k), h, *index[h])]
            if k:
                got(own, recv_s.at[j, 0, h, 15])
            for d in (2, 1, 3):
                put(own, own, send_s.at[j, k, h, 6 + d], recv_s.at[j, k, h, 6 + d], devs[h][1](d))

    def wb(j, k):
        for h in range(2):
            i1, i2 = index[h]
            for d in range(1, 4):
                got(wbuf.at[at(j, side(k), h, i1, (i2 + 4 - d) % 4)], recv_s.at[j, k, h, 6 + d])
            own = wbuf.at[at(j, side(k), h, i1)]
            for n, d in enumerate((1, 3)):
                put(own, own, send_s.at[j, k, h, 10 + n], recv_s.at[j, k, h, 10 + n], devs[h][0](d))

    def wc(j, k):
        for h in range(2):
            i1 = index[h][0]
            for n, (d, part) in enumerate(((1, LOW), (3, HIGH))):
                back = (i1 + 4 - d) % 4
                got(wbuf.at[at(j, side(k), h, back)], recv_s.at[j, k, h, 10 + n])
                piece = wbuf.at[at(j, side(k), h, back, part)]
                put(piece, piece, send_s.at[j, k, h, 12 + n], recv_s.at[j, k, h, 12 + n], devs[h][0](d))

    def wd(j, k):
        for h in range(2):
            far = (index[h][0] + 2) % 4
            for n, part in enumerate((LOW, HIGH)):
                got(wbuf.at[at(j, side(k), h, far, part)], recv_s.at[j, k, h, 12 + n])

        def times(rows, h):
            return jnp.dot(
                hbuf[j, side(k), rows], wbuf[j, side(k), h].reshape(512, HALF), preferred_element_type=F32
            )

        if (j, k) != (NJ - 1, 1):

            @pl.loop(0, 4)
            def _(b):
                rows = pl.ds(pl.multiple_of(b * 256, 256), 256)
                for h in range(2):
                    cols = slice(h * HALF, (h + 1) * HALF)
                    if (j, k) == (0, 0):
                        acc[rows, cols] = times(rows, h)
                    else:
                        acc[rows, cols] += times(rows, h)
        else:
            for b in range(4):
                core = 1 - c if b < 2 else c
                rows = pl.ds(pl.multiple_of(core * 512 + (b % 2) * 256, 256), 256)
                for h in range(2):
                    cols = slice(h * HALF, (h + 1) * HALF)
                    part = acc[rows, cols] + times(rows, h)
                    if b < 2:
                        fsend[b, :, cols] = part.astype(BF16)
                    else:
                        acc[rows, cols] = part
                if b < 2:
                    put(fsend.at[b], frecv.at[b], small_s.at[12 + b], small_r.at[12 + b], sib)

    def last():
        for b in range(2):
            got(frecv.at[b], small_r.at[12 + b])
            rows = pl.ds(pl.multiple_of(c * 512 + b * 256, 256), 256)
            fresh_out[b * 256 : (b + 1) * 256] = (acc[rows] + frecv[b].astype(F32)).astype(BF16)

    for stage, j, x in schedule():
        if stage == "g0":
            g0(j, x)
        elif stage == "g1":
            g1(j, x)
        elif stage == "g2":
            g2(j, x)
        elif stage == "g3":
            g3(j, x)
        elif stage == "gx":
            gx(j)
        elif stage == "gy":
            gy(j)
        elif stage == "gg":
            gg(j)
        elif stage == "wa":
            wa(j, x)
        elif stage == "wb":
            wb(j, x)
        elif stage == "wc":
            wc(j, x)
        elif stage == "wd":
            wd(j, x)
        else:
            last()

    for j in range(NJ):
        for d in range(1, 4):
            got(g_out.at[j, (y + 4 - d) % 4], gg_r.at[j, d - 1])
        for x in range(2):
            for k in range(3):
                whole = hbuf.at[j, x, mine]
                pltpu.make_async_remote_copy(
                    whole, whole, h_s.at[j, x, k], h_s.at[j, x, k], device_id=sib, device_id_type=MESH
                ).wait_send()
    for copy in sends:
        copy.wait_send()


def finish_kernel(g, count, master, first, second, fresh, new_master, new_first, new_second, fresh_out):
    rows = master.shape[0]
    summed = g[...].astype(F32).reshape(rows, 8, 128)
    grad = summed / jnp.broadcast_to(count[...][0:1, 0:1].reshape(1, 1, 1), (rows, 8, 128))
    a, b, d = adamw(master[...], first[...], second[...], grad)
    new_master[...] = a
    new_first[...] = b
    new_second[...] = d
    fresh_out[...] = fresh[...].astype(F32).reshape(rows, 8, 128).astype(BF16)


def tiles(array):
    n = array.shape[0]
    return array.reshape(n, 2, 4, 128).transpose(0, 2, 1, 3).reshape(n, 8, 128)


def untiles(array):
    n = array.shape[0]
    return array.reshape(n, 4, 2, 128).transpose(0, 2, 1, 3).reshape(n, 2, 512)


def local(hidden_in, lengths, kv_grad_out, master, moment_one, moment_two):
    kv = tiles(kv_grad_out)
    states = [tiles(a) for a in (master, moment_one, moment_two)]
    hbm = pl.BlockSpec(memory_space=pl.ANY)
    vmem = pl.BlockSpec(memory_space=pltpu.VMEM)
    dma = pltpu.SemaphoreType.DMA
    fresh, g, count = pl.pallas_call(
        main_kernel,
        out_shape=(
            jax.ShapeDtypeStruct((TOK, FEAT), BF16),
            jax.ShapeDtypeStruct((NJ, 4, 32, FEAT), BF16),
            jax.ShapeDtypeStruct((8, 128), F32),
        ),
        in_specs=[hbm, pl.BlockSpec(memory_space=pltpu.SMEM), hbm, hbm, hbm, hbm],
        out_specs=(vmem, vmem, vmem),
        scratch_shapes=[
            pltpu.VMEM((NJ, 2, 1024, 512), BF16),
            pltpu.VMEM((1024, FEAT), BF16),
            pltpu.VMEM((TOK, 8, 128), BF16),
            pltpu.VMEM((NJ, 2, 2, 4, 4, 32, HALF), BF16),
            pltpu.VMEM((NJ, 2, 2, 2, 2, 32, HALF), BF16),
            pltpu.VMEM((NJ, 2, 2, 2, 4, 32, HALF), BF16),
            pltpu.VMEM((NJ, 2, 2, 3, 32, HALF), BF16),
            pltpu.VMEM((NJ, 2, 32, HALF), BF16),
            pltpu.VMEM((NJ, 2, 2, 4, 4, 32, HALF), BF16),
            pltpu.VMEM((1024, FEAT), F32),
            pltpu.VMEM((2, 256, FEAT), BF16),
            pltpu.VMEM((2, 256, FEAT), BF16),
            pltpu.VMEM((3, NJ, 32, 8, 128), F32),
            pltpu.VMEM((12, 8, 128), F32),
            dma((NJ, 2, 2, 16)),
            dma((NJ, 2, 2, 16)),
            dma((NJ, 3)),
            dma((NJ, 3)),
            dma((NJ, 2, 3)),
            dma((NJ, 2, 4)),
            dma((NJ, 2)),
            dma((14,)),
            dma((14,)),
            dma((4 + 3 * NJ,)),
        ],
        compiler_params=pltpu.CompilerParams(
            collective_id=0, has_side_effects=True, vmem_limit_bytes=50 * 2**20
        ),
        name="project",
    )(hidden_in, lengths, kv, *states)
    g = g.reshape(TOK, FEAT)
    step = 64
    flat = pl.BlockSpec((step, FEAT), lambda i: (i, 0))
    cube = pl.BlockSpec((step, 8, 128), lambda i: (i, 0, 0))
    outs = pl.pallas_call(
        finish_kernel,
        grid=(TOK // step,),
        out_shape=[jax.ShapeDtypeStruct((TOK, 8, 128), F32)] * 3
        + [jax.ShapeDtypeStruct((TOK, 8, 128), BF16)],
        in_specs=[flat, pl.BlockSpec((8, 128), lambda i: (0, 0)), cube, cube, cube, flat],
        out_specs=[cube] * 4,
        compiler_params=pltpu.CompilerParams(vmem_limit_bytes=24 * 2**20),
        name="update",
    )(g, count, *states, fresh)
    return tuple(untiles(a) for a in outs)


def solution(mesh):
    in_specs = (
        P(("rep", "shard", "tp"), None),
        P(("rep", "shard")),
        P(("rep", "shard"), None, "tp"),
        P("shard", None, "tp"),
        P("shard", None, "tp"),
        P("shard", None, "tp"),
    )
    out_specs = (
        P("shard", None, "tp"),
        P("shard", None, "tp"),
        P("shard", None, "tp"),
        P(("rep", "shard"), None, "tp"),
    )
    return jax.shard_map(local, mesh=mesh, in_specs=in_specs, out_specs=out_specs, check_vma=False)
```

```python
import functools

import jax
import jax.numpy as jnp
from jax import lax
from jax.experimental import pallas as pl
from jax.experimental.pallas import tpu as pltpu
from jax.sharding import PartitionSpec as P

MESH = pl.DeviceIdType.MESH
F32, BF16 = jnp.float32, jnp.bfloat16

beta_one = 0.9
beta_two = 0.95
step_count = 20
rate = 0.002
decay = 0.1
epsilon = 1e-08

AHEAD = 7
NJ = 4
TOK = 512
FEAT = 1024
HALF = 512


def schedule():
    order = []

    def add(stage, j, x=0):
        if 0 <= j < NJ:
            order.append((stage, j, x))

    def send(m, n):
        if m < 2 * NJ:
            order.append(("h", 4 * m + n + AHEAD, 0))

    for i in range(NJ + 1):
        add("g2", i - 1, 1)
        add("g0", i, 0)
        add("wc", i - 2, 1)
        add("g3", i - 1, 1)
        add("gx", i - 1, 0)
        send(2 * i, 1)
        add("g1", i, 0)
        add("wd", i - 2, 0)
        send(2 * i, 2)
        add("wd", i - 2, 1)
        add("gy", i - 1, 0)
        add("gg", i - 1, 0)
        add("g2", i, 0)
        send(2 * i, 3)
        add("g0", i, 1)
        add("wa", i - 1, 1)
        add("wb", i - 1, 0)
        send(2 * i + 1, 1)
        add("g1", i, 1)
        add("g3", i, 0)
        send(2 * i + 1, 2)
        add("wb", i - 1, 1)
        add("wc", i - 1, 0)
        send(2 * i + 1, 3)
    for n in range(4):
        order.insert(order.index(("g%d" % min(n, 3), 0, 0 if n < 3 else 1)) + 1, ("count", 0, n))
    j = NJ - 1
    return order + [("wc", j, 1), ("wd", j, 0), ("wd", j, 1), ("last", 0, 0)]


def adamw(master, moment_one, moment_two, grad):
    first = beta_one * moment_one + (1.0 - beta_one) * grad
    second = beta_two * moment_two + (1.0 - beta_two) * grad * grad
    first_hat = first * (1.0 / (1.0 - beta_one**step_count))
    second_hat = second * (1.0 / (1.0 - beta_two**step_count))
    updated = master - rate * (first_hat / (jnp.sqrt(second_hat) + epsilon) + decay * master)
    return (updated, first, second)


def main_kernel(
    hid,
    lengths,
    kv,
    master,
    first,
    second,
    fresh_out,
    g_out,
    count_out,
    hbuf,
    cbuf,
    kvbuf,
    gbuf,
    r1,
    r2,
    r3,
    r4,
    wbuf,
    acc,
    fsend,
    frecv,
    mbuf,
    cnt,
    send_s,
    recv_s,
    gg_s,
    gg_r,
    h_s,
    h_r,
    h_l,
    small_s,
    small_r,
    load_s,
):
    y = lax.axis_index("rep")
    s = lax.axis_index("shard")
    t = lax.axis_index("tp")
    z = s // 4
    xl = (s // 2) % 2
    c = s % 2

    def ydev(d):
        return ((y + d) % 4, s, t)

    def zdev(d):
        return (y, ((z + d) % 4) * 4 + s % 4, t)

    xdev = (y, z * 4 + (1 - xl) * 2 + c, t)
    sib = (y, z * 4 + xl * 2 + (1 - c), t)

    def partner(core):
        return (y, z * 4 + xl * 2 + core, 1 - t)

    peers = [ydev(1), ydev(2), ydev(3), zdev(1), zdev(2), zdev(3), xdev, sib, partner(0), partner(1)]
    sends = []

    def put(src, dst, ss, rs, dev):
        copy = pltpu.make_async_remote_copy(src, dst, ss, rs, device_id=dev, device_id_type=MESH)
        copy.start()
        sends.append(copy)

    def got(dst, rs):
        pltpu.make_async_remote_copy(dst, dst, rs, rs, device_id=sib, device_id_type=MESH).wait_recv()

    mine = pl.ds(pl.multiple_of(c * 512 + t * 256, 256), 256)

    def columns(j, x, n, core):
        return pl.ds(pl.multiple_of((4 * n + 2 * x + core) * 512 + j * 128, 128), 128)

    def lanes(n):
        return pl.ds(pl.multiple_of(n * 128, 128), 128)

    def h_local(j, x):
        @pl.loop(0, 4)
        def _(n):
            pltpu.make_async_copy(
                hid.at[:, columns(j, x, n, c)], hbuf.at[j, x, mine, lanes(n)], h_l.at[j, x]
            ).start()

    def h_send(quarter):
        m, n = divmod(quarter, 4)
        if m >= 2 * NJ:
            return
        j, x = divmod(m, 2)
        for k, (dev, core) in enumerate(((partner(0), 0), (partner(1), 1), (sib, 1 - c))):
            pltpu.make_async_remote_copy(
                hid.at[:, columns(j, x, n, core)],
                hbuf.at[j, x, mine, lanes(n)],
                h_s.at[j, x, k],
                h_r.at[j, x, c * 2 + t],
                device_id=dev,
                device_id_type=MESH,
            ).start()

    def h_wait(j, x):
        pltpu.make_async_copy(hbuf.at[j, x, mine], hbuf.at[j, x, mine], h_l.at[j, x]).wait()
        for core, tp in ((1 - c, t), (0, 1 - t), (1, 1 - t)):
            rows = pl.ds(pl.multiple_of(core * 512 + tp * 256, 256), 256)
            got(hbuf.at[j, x, rows], h_r.at[j, x, core * 2 + tp])

    barrier = pltpu.get_barrier_semaphore()
    for dev in peers:
        pl.semaphore_signal(barrier, inc=1, device_id=dev, device_id_type=MESH)
    pl.semaphore_wait(barrier, len(peers))

    for quarter in range(4):
        h_send(quarter)

    kv_load = pltpu.make_async_copy(kv, kvbuf, load_s.at[3])
    kv_load.start()
    for m in range(2 * NJ):
        h_local(m // 2, m % 2)
    loads = []
    for k, ref in enumerate((master, first, second)):
        for j in range(NJ):
            loads.append(
                pltpu.make_async_copy(
                    ref.at[pl.ds(j * 128 + y * 32, 32)], mbuf.at[k, j], load_s.at[4 + k * NJ + j]
                )
            )
    for load in loads:
        load.start()

    def count_step(base, n, me, devs, sem):
        for d in range(1, n):
            put(cnt.at[base + me], cnt.at[base + me], small_s.at[sem + d], small_r.at[sem + d], devs(d))

    def count_sum(base, n, me, sem):
        for d in range(1, n):
            got(cnt.at[base + (me + n - d) % n], small_r.at[sem + d])
        total = cnt[base]
        for d in range(1, n):
            total = total + cnt[base + d]
        return total

    cnt[y] = jnp.full((8, 128), lengths[0], jnp.int32).astype(F32)
    count_step(0, 4, y, ydev, 0)

    kv_load.wait()

    @pl.loop(0, 8)
    def _(b):
        rows = pl.ds(pl.multiple_of(b * 64, 64), 64)
        value = kvbuf[rows].astype(F32)
        token = lax.broadcasted_iota(jnp.int32, (64, 8, 128), 0) + b * 64
        value = jnp.where(token < lengths[0], value, 0.0)
        cbuf[pl.ds(pl.multiple_of(c * 512 + b * 64, 64), 64)] = value.reshape(64, FEAT).astype(BF16)

    own_c = cbuf.at[pl.ds(pl.multiple_of(c * 512, 512), 512)]
    sib_c = cbuf.at[pl.ds(pl.multiple_of((1 - c) * 512, 512), 512)]
    put(own_c, own_c, small_s.at[0], small_r.at[0], sib)

    for quarter in range(4, AHEAD):
        h_send(quarter)
    got(sib_c, small_r.at[0])

    index = ((y, z), (z, y))
    devs = ((ydev, zdev), (zdev, ydev))
    every = slice(None)
    LOW, HIGH = pl.ds(0, 2), pl.ds(2, 2)

    def at(j, x, h, a1, a2=every):
        return (j, x, h, a2, a1) if h == 0 else (j, x, h, a1, a2)

    def g0(j, x):
        h_wait(j, x)
        h_send(8 * j + 4 * x + AHEAD)

        @pl.loop(0, 2)
        def _(n):
            left = hbuf[j, x, :, pl.ds(pl.multiple_of(n * 256, 256), 256)]
            pair = pl.ds(n * 2, 2)
            for h in range(2):
                part = lax.dot_general(
                    left,
                    cbuf[:, h * HALF : (h + 1) * HALF],
                    (((0,), (0,)), ((), ())),
                    preferred_element_type=F32,
                )
                gbuf[j, x, h, pair] = part.astype(BF16).reshape(2, 4, 32, HALF)

        for h in range(2):
            far = (index[h][0] + 2) % 4
            for k, (d, part) in enumerate(((1, LOW), (3, HIGH))):
                put(
                    gbuf.at[at(j, x, h, far, part)],
                    r1.at[j, x, h, k],
                    send_s.at[j, x, h, k],
                    recv_s.at[j, x, h, k],
                    devs[h][0](d),
                )

    def g1(j, x):
        for h in range(2):
            i1 = index[h][0]
            for k, (d, low) in enumerate(((1, 0), (3, 2))):
                got(r1.at[j, x, h, k], recv_s.at[j, x, h, k])
                to = (i1 + d) % 4
                for a in range(2):
                    spot = at(j, x, h, to, low + a)
                    gbuf[spot] = (gbuf[spot].astype(F32) + r1[j, x, h, k, a].astype(F32)).astype(BF16)
                put(
                    gbuf.at[at(j, x, h, to)],
                    r2.at[j, x, h, k],
                    send_s.at[j, x, h, 2 + k],
                    recv_s.at[j, x, h, 2 + k],
                    devs[h][0](d),
                )

    def g2(j, x):
        for h in range(2):
            i1, i2 = index[h]
            for k in range(2):
                got(r2.at[j, x, h, k], recv_s.at[j, x, h, 2 + k])
            for d in (2, 1, 3, 0):
                a2 = (i2 + d) % 4
                spot = at(j, x, h, i1, a2)
                gbuf[spot] = (
                    gbuf[spot].astype(F32) + r2[j, x, h, 0, a2].astype(F32) + r2[j, x, h, 1, a2].astype(F32)
                ).astype(BF16)
                if d:
                    put(
                        gbuf.at[spot],
                        r3.at[j, x, h, d - 1],
                        send_s.at[j, x, h, 3 + d],
                        recv_s.at[j, x, h, 3 + d],
                        devs[h][1](d),
                    )

    def g3(j, x):
        for h in range(2):
            i1, i2 = index[h]
            for d in range(1, 4):
                got(r3.at[j, x, h, d - 1], recv_s.at[j, x, h, 3 + d])
            spot = at(j, x, h, i1, i2)
            total = gbuf[spot].astype(F32)
            for d in range(3):
                total = total + r3[j, x, h, d].astype(F32)
            gbuf[spot] = total.astype(BF16)

    def gx(j):
        for h in range(2):
            put(gbuf.at[at(j, 1 - xl, h, *index[h])], r4.at[j, h], send_s.at[j, 0, h, 14], recv_s.at[j, 0, h, 14], xdev)

    def gy(j):
        for k in range(3):
            loads[k * NJ + j].wait()
        inverse = jnp.broadcast_to(1.0 / count_out[0:1, 0:1], (32, FEAT))
        halves = []
        for h in range(2):
            got(r4.at[j, h], recv_s.at[j, 0, h, 14])
            halves.append(gbuf[at(j, xl, h, *index[h])].astype(F32) + r4[j, h].astype(F32))
        summed = jnp.concatenate(halves, axis=1).astype(BF16)
        g_out[j, y] = summed
        grad = summed.astype(F32) * inverse
        new, _, _ = adamw(*(mbuf[k, j].reshape(32, FEAT) for k in range(3)), grad)
        new = new.astype(BF16)
        for h in range(2):
            spot = at(j, xl, h, *index[h])
            wbuf[spot] = new[:, h * HALF : (h + 1) * HALF]
            own = wbuf.at[spot]
            put(own, own, send_s.at[j, 0, h, 15], recv_s.at[j, 0, h, 15], xdev)
        wa(j, 0)

    def gg(j):
        for d in range(1, 4):
            put(g_out.at[j, y], g_out.at[j, y], gg_s.at[j, d - 1], gg_r.at[j, d - 1], ydev(d))

    def side(k):
        return 1 - xl if k else xl

    def wa(j, k):
        for h in range(2):
            own = wbuf.at[at(j, side(k), h, *index[h])]
            if k:
                got(own, recv_s.at[j, 0, h, 15])
            for d in (2, 1, 3):
                put(own, own, send_s.at[j, k, h, 6 + d], recv_s.at[j, k, h, 6 + d], devs[h][1](d))

    def wb(j, k):
        for h in range(2):
            i1, i2 = index[h]
            for d in range(1, 4):
                got(wbuf.at[at(j, side(k), h, i1, (i2 + 4 - d) % 4)], recv_s.at[j, k, h, 6 + d])
            own = wbuf.at[at(j, side(k), h, i1)]
            for n, d in enumerate((1, 3)):
                put(own, own, send_s.at[j, k, h, 10 + n], recv_s.at[j, k, h, 10 + n], devs[h][0](d))

    def wc(j, k):
        for h in range(2):
            i1 = index[h][0]
            for n, (d, part) in enumerate(((1, LOW), (3, HIGH))):
                back = (i1 + 4 - d) % 4
                got(wbuf.at[at(j, side(k), h, back)], recv_s.at[j, k, h, 10 + n])
                piece = wbuf.at[at(j, side(k), h, back, part)]
                put(piece, piece, send_s.at[j, k, h, 12 + n], recv_s.at[j, k, h, 12 + n], devs[h][0](d))

    def wd(j, k):
        for h in range(2):
            far = (index[h][0] + 2) % 4
            for n, part in enumerate((LOW, HIGH)):
                got(wbuf.at[at(j, side(k), h, far, part)], recv_s.at[j, k, h, 12 + n])

        def times(rows, h):
            return jnp.dot(
                hbuf[j, side(k), rows], wbuf[j, side(k), h].reshape(512, HALF), preferred_element_type=F32
            )

        if (j, k) != (NJ - 1, 1):

            @pl.loop(0, 4)
            def _(b):
                rows = pl.ds(pl.multiple_of(b * 256, 256), 256)
                for h in range(2):
                    cols = slice(h * HALF, (h + 1) * HALF)
                    if (j, k) == (0, 0):
                        acc[rows, cols] = times(rows, h)
                    else:
                        acc[rows, cols] += times(rows, h)
        else:
            for b in range(4):
                core = 1 - c if b < 2 else c
                rows = pl.ds(pl.multiple_of(core * 512 + (b % 2) * 256, 256), 256)
                for h in range(2):
                    cols = slice(h * HALF, (h + 1) * HALF)
                    part = acc[rows, cols] + times(rows, h)
                    if b < 2:
                        fsend[b, :, cols] = part.astype(BF16)
                    else:
                        acc[rows, cols] = part
                if b < 2:
                    put(fsend.at[b], frecv.at[b], small_s.at[12 + b], small_r.at[12 + b], sib)

    def last():
        for b in range(2):
            got(frecv.at[b], small_r.at[12 + b])
            rows = pl.ds(pl.multiple_of(c * 512 + b * 256, 256), 256)
            fresh_out[b * 256 : (b + 1) * 256] = (acc[rows] + frecv[b].astype(F32)).astype(BF16)

    def count_stage(n):
        if n == 0:
            cnt[4 + z] = count_sum(0, 4, y, 0)
            count_step(4, 4, z, zdev, 4)
        elif n == 1:
            cnt[8 + xl] = count_sum(4, 4, z, 4)
            count_step(8, 2, xl, lambda d: xdev, 8)
        elif n == 2:
            cnt[10 + c] = count_sum(8, 2, xl, 8)
            count_step(10, 2, c, lambda d: sib, 10)
        else:
            count_out[...] = count_sum(10, 2, c, 10)

    for stage, j, x in schedule():
        if stage == "g0":
            g0(j, x)
        elif stage == "g1":
            g1(j, x)
        elif stage == "g2":
            g2(j, x)
        elif stage == "g3":
            g3(j, x)
        elif stage == "gx":
            gx(j)
        elif stage == "gy":
            gy(j)
        elif stage == "gg":
            gg(j)
        elif stage == "wa":
            wa(j, x)
        elif stage == "wb":
            wb(j, x)
        elif stage == "wc":
            wc(j, x)
        elif stage == "wd":
            wd(j, x)
        elif stage == "h":
            h_send(j)
        elif stage == "count":
            count_stage(x)
        else:
            last()

    for j in range(NJ):
        for d in range(1, 4):
            got(g_out.at[j, (y + 4 - d) % 4], gg_r.at[j, d - 1])
        for x in range(2):
            for k in range(3):
                whole = hbuf.at[j, x, mine]
                pltpu.make_async_remote_copy(
                    whole, whole, h_s.at[j, x, k], h_s.at[j, x, k], device_id=sib, device_id_type=MESH
                ).wait_send()
    for copy in sends:
        copy.wait_send()


def finish_kernel(g, count, master, first, second, fresh, new_master, new_first, new_second, fresh_out):
    rows = master.shape[0]
    summed = g[...].astype(F32).reshape(rows, 8, 128)
    grad = summed * jnp.broadcast_to((1.0 / count[...])[0:1, 0:1].reshape(1, 1, 1), (rows, 8, 128))
    a, b, d = adamw(master[...], first[...], second[...], grad)
    new_master[...] = a
    new_first[...] = b
    new_second[...] = d
    fresh_out[...] = fresh[...].astype(F32).reshape(rows, 8, 128).astype(BF16)


def tiles(array):
    n = array.shape[0]
    return array.reshape(n, 2, 4, 128).transpose(0, 2, 1, 3).reshape(n, 8, 128)


def untiles(array):
    n = array.shape[0]
    return array.reshape(n, 4, 2, 128).transpose(0, 2, 1, 3).reshape(n, 2, 512)


def local(hidden_in, lengths, kv_grad_out, master, moment_one, moment_two):
    kv = tiles(kv_grad_out)
    states = [tiles(a) for a in (master, moment_one, moment_two)]
    hbm = pl.BlockSpec(memory_space=pl.ANY)
    vmem = pl.BlockSpec(memory_space=pltpu.VMEM)
    dma = pltpu.SemaphoreType.DMA
    fresh, g, count = pl.pallas_call(
        main_kernel,
        out_shape=(
            jax.ShapeDtypeStruct((TOK, FEAT), BF16),
            jax.ShapeDtypeStruct((NJ, 4, 32, FEAT), BF16),
            jax.ShapeDtypeStruct((8, 128), F32),
        ),
        in_specs=[hbm, pl.BlockSpec(memory_space=pltpu.SMEM), pl.BlockSpec(memory_space=pltpu.HBM), hbm, hbm, hbm],
        out_specs=(vmem, vmem, vmem),
        scratch_shapes=[
            pltpu.VMEM((NJ, 2, 1024, 512), BF16),
            pltpu.VMEM((1024, FEAT), BF16),
            pltpu.VMEM((TOK, 8, 128), BF16),
            pltpu.VMEM((NJ, 2, 2, 4, 4, 32, HALF), BF16),
            pltpu.VMEM((NJ, 2, 2, 2, 2, 32, HALF), BF16),
            pltpu.VMEM((NJ, 2, 2, 2, 4, 32, HALF), BF16),
            pltpu.VMEM((NJ, 2, 2, 3, 32, HALF), BF16),
            pltpu.VMEM((NJ, 2, 32, HALF), BF16),
            pltpu.VMEM((NJ, 2, 2, 4, 4, 32, HALF), BF16),
            pltpu.VMEM((1024, FEAT), F32),
            pltpu.VMEM((2, 256, FEAT), BF16),
            pltpu.VMEM((2, 256, FEAT), BF16),
            pltpu.VMEM((3, NJ, 32, 8, 128), F32),
            pltpu.VMEM((12, 8, 128), F32),
            dma((NJ, 2, 2, 16)),
            dma((NJ, 2, 2, 16)),
            dma((NJ, 3)),
            dma((NJ, 3)),
            dma((NJ, 2, 3)),
            dma((NJ, 2, 4)),
            dma((NJ, 2)),
            dma((14,)),
            dma((14,)),
            dma((4 + 3 * NJ,)),
        ],
        compiler_params=pltpu.CompilerParams(
            collective_id=0, has_side_effects=True, vmem_limit_bytes=50 * 2**20
        ),
        name="project",
    )(hidden_in, lengths, kv, *states)
    g = g.reshape(TOK, FEAT)
    step = 64
    flat = pl.BlockSpec((step, FEAT), lambda i: (i, 0))
    cube = pl.BlockSpec((step, 8, 128), lambda i: (i, 0, 0))
    outs = pl.pallas_call(
        finish_kernel,
        grid=(TOK // step,),
        out_shape=[jax.ShapeDtypeStruct((TOK, 8, 128), F32)] * 3
        + [jax.ShapeDtypeStruct((TOK, 8, 128), BF16)],
        in_specs=[flat, pl.BlockSpec((8, 128), lambda i: (0, 0)), cube, cube, cube, flat],
        out_specs=[cube] * 4,
        compiler_params=pltpu.CompilerParams(vmem_limit_bytes=24 * 2**20),
        name="update",
    )(g, count, *states, fresh)
    return tuple(untiles(a) for a in outs)


def solution(mesh):
    in_specs = (
        P(("rep", "shard", "tp"), None),
        P(("rep", "shard")),
        P(("rep", "shard"), None, "tp"),
        P("shard", None, "tp"),
        P("shard", None, "tp"),
        P("shard", None, "tp"),
    )
    out_specs = (
        P("shard", None, "tp"),
        P("shard", None, "tp"),
        P("shard", None, "tp"),
        P(("rep", "shard"), None, "tp"),
    )
    return jax.shard_map(local, mesh=mesh, in_specs=in_specs, out_specs=out_specs, check_vma=False)
```

```python
import functools

import jax
import jax.numpy as jnp
from jax import lax
from jax.experimental import pallas as pl
from jax.experimental.pallas import tpu as pltpu
from jax.sharding import PartitionSpec as P

MESH = pl.DeviceIdType.MESH
F32, BF16 = jnp.float32, jnp.bfloat16

beta_one = 0.9
beta_two = 0.95
step_count = 20
rate = 0.002
decay = 0.1
epsilon = 1e-08

AHEAD = 7
NJ = 4
TOK = 512
FEAT = 1024
HALF = 512


def schedule():
    order = []

    def add(stage, j, x=0):
        if 0 <= j < NJ:
            order.append((stage, j, x))

    def send(m, n):
        if m < 2 * NJ:
            order.append(("h", 4 * m + n + AHEAD, 0))

    for i in range(NJ + 1):
        add("g2", i - 1, 1)
        add("g0", i, 0)
        add("wc", i - 2, 1)
        add("g3", i - 1, 1)
        add("gx", i - 1, 0)
        send(2 * i, 1)
        add("g1", i, 0)
        add("wd", i - 2, 0)
        send(2 * i, 2)
        add("gy", i - 1, 0)
        add("gg", i - 1, 0)
        add("g2", i, 0)
        send(2 * i, 3)
        add("g0", i, 1)
        add("wd", i - 2, 1)
        add("wa", i - 1, 1)
        add("wb", i - 1, 0)
        send(2 * i + 1, 1)
        add("g1", i, 1)
        add("g3", i, 0)
        send(2 * i + 1, 2)
        add("wb", i - 1, 1)
        add("wc", i - 1, 0)
        send(2 * i + 1, 3)
    for n in range(4):
        order.insert(order.index(("g%d" % min(n, 3), 0, 0 if n < 3 else 1)) + 1, ("count", 0, n))
    j = NJ - 1
    return order + [("wc", j, 1), ("wd", j, 0), ("wd", j, 1), ("last", 0, 0)]


def adamw(master, moment_one, moment_two, grad):
    first = beta_one * moment_one + (1.0 - beta_one) * grad
    second = beta_two * moment_two + (1.0 - beta_two) * grad * grad
    first_hat = first * (1.0 / (1.0 - beta_one**step_count))
    second_hat = second * (1.0 / (1.0 - beta_two**step_count))
    updated = master - rate * (first_hat / (jnp.sqrt(second_hat) + epsilon) + decay * master)
    return (updated, first, second)


def main_kernel(
    hid,
    lengths,
    kv,
    master,
    first,
    second,
    fresh_out,
    g_out,
    count_out,
    hbuf,
    cbuf,
    kvbuf,
    gbuf,
    r1,
    r2,
    r3,
    r4,
    wbuf,
    acc,
    fsend,
    frecv,
    mbuf,
    cnt,
    send_s,
    recv_s,
    gg_s,
    gg_r,
    h_s,
    h_r,
    h_l,
    small_s,
    small_r,
    load_s,
):
    y = lax.axis_index("rep")
    s = lax.axis_index("shard")
    t = lax.axis_index("tp")
    z = s // 4
    xl = (s // 2) % 2
    c = s % 2

    def ydev(d):
        return ((y + d) % 4, s, t)

    def zdev(d):
        return (y, ((z + d) % 4) * 4 + s % 4, t)

    xdev = (y, z * 4 + (1 - xl) * 2 + c, t)
    sib = (y, z * 4 + xl * 2 + (1 - c), t)

    def partner(core):
        return (y, z * 4 + xl * 2 + core, 1 - t)

    peers = [ydev(1), ydev(2), ydev(3), zdev(1), zdev(2), zdev(3), xdev, sib, partner(0), partner(1)]
    sends = []

    def put(src, dst, ss, rs, dev):
        copy = pltpu.make_async_remote_copy(src, dst, ss, rs, device_id=dev, device_id_type=MESH)
        copy.start()
        sends.append(copy)

    def got(dst, rs):
        pltpu.make_async_remote_copy(dst, dst, rs, rs, device_id=sib, device_id_type=MESH).wait_recv()

    mine = pl.ds(pl.multiple_of(c * 512 + t * 256, 256), 256)

    def columns(j, x, n, core):
        return pl.ds(pl.multiple_of((4 * n + 2 * x + core) * 512 + j * 128, 128), 128)

    def lanes(n):
        return pl.ds(pl.multiple_of(n * 128, 128), 128)

    def h_local(j, x):
        @pl.loop(0, 4)
        def _(n):
            pltpu.make_async_copy(
                hid.at[:, columns(j, x, n, c)], hbuf.at[j, x, mine, lanes(n)], h_l.at[j, x]
            ).start()

    def h_send(quarter):
        m, n = divmod(quarter, 4)
        if m >= 2 * NJ:
            return
        j, x = divmod(m, 2)
        for k, (dev, core) in enumerate(((partner(0), 0), (partner(1), 1), (sib, 1 - c))):
            pltpu.make_async_remote_copy(
                hid.at[:, columns(j, x, n, core)],
                hbuf.at[j, x, mine, lanes(n)],
                h_s.at[j, x, k],
                h_r.at[j, x, c * 2 + t],
                device_id=dev,
                device_id_type=MESH,
            ).start()

    def h_wait(j, x):
        pltpu.make_async_copy(hbuf.at[j, x, mine], hbuf.at[j, x, mine], h_l.at[j, x]).wait()
        for core, tp in ((1 - c, t), (0, 1 - t), (1, 1 - t)):
            rows = pl.ds(pl.multiple_of(core * 512 + tp * 256, 256), 256)
            got(hbuf.at[j, x, rows], h_r.at[j, x, core * 2 + tp])

    barrier = pltpu.get_barrier_semaphore()
    for dev in peers:
        pl.semaphore_signal(barrier, inc=1, device_id=dev, device_id_type=MESH)
    pl.semaphore_wait(barrier, len(peers))

    for quarter in range(4):
        h_send(quarter)

    kv_load = pltpu.make_async_copy(kv, kvbuf, load_s.at[3])
    kv_load.start()
    for m in range(2 * NJ):
        h_local(m // 2, m % 2)
    loads = []
    for k, ref in enumerate((master, first, second)):
        for j in range(NJ):
            loads.append(
                pltpu.make_async_copy(
                    ref.at[pl.ds(j * 128 + y * 32, 32)], mbuf.at[k, j], load_s.at[4 + k * NJ + j]
                )
            )
    for load in loads:
        load.start()

    def count_step(base, n, me, devs, sem):
        for d in range(1, n):
            put(cnt.at[base + me], cnt.at[base + me], small_s.at[sem + d], small_r.at[sem + d], devs(d))

    def count_sum(base, n, me, sem):
        for d in range(1, n):
            got(cnt.at[base + (me + n - d) % n], small_r.at[sem + d])
        total = cnt[base]
        for d in range(1, n):
            total = total + cnt[base + d]
        return total

    cnt[y] = jnp.full((8, 128), lengths[0], jnp.int32).astype(F32)
    count_step(0, 4, y, ydev, 0)

    kv_load.wait()

    @pl.loop(0, 8)
    def _(b):
        rows = pl.ds(pl.multiple_of(b * 64, 64), 64)
        value = kvbuf[rows].astype(F32)
        token = lax.broadcasted_iota(jnp.int32, (64, 8, 128), 0) + b * 64
        value = jnp.where(token < lengths[0], value, 0.0)
        cbuf[pl.ds(pl.multiple_of(c * 512 + b * 64, 64), 64)] = value.reshape(64, FEAT).astype(BF16)

    own_c = cbuf.at[pl.ds(pl.multiple_of(c * 512, 512), 512)]
    sib_c = cbuf.at[pl.ds(pl.multiple_of((1 - c) * 512, 512), 512)]
    put(own_c, own_c, small_s.at[0], small_r.at[0], sib)

    for quarter in range(4, AHEAD):
        h_send(quarter)
    got(sib_c, small_r.at[0])

    index = ((y, z), (z, y))
    devs = ((ydev, zdev), (zdev, ydev))
    every = slice(None)
    LOW, HIGH = pl.ds(0, 2), pl.ds(2, 2)

    def at(j, x, h, a1, a2=every):
        return (j, x, h, a2, a1) if h == 0 else (j, x, h, a1, a2)

    def g0(j, x):
        h_wait(j, x)
        h_send(8 * j + 4 * x + AHEAD)

        @pl.loop(0, 2)
        def _(n):
            left = hbuf[j, x, :, pl.ds(pl.multiple_of(n * 256, 256), 256)]
            pair = pl.ds(n * 2, 2)
            for h in range(2):
                part = lax.dot_general(
                    left,
                    cbuf[:, h * HALF : (h + 1) * HALF],
                    (((0,), (0,)), ((), ())),
                    preferred_element_type=F32,
                )
                gbuf[j, x, h, pair] = part.astype(BF16).reshape(2, 4, 32, HALF)

        for h in range(2):
            far = (index[h][0] + 2) % 4
            for k, (d, part) in enumerate(((1, LOW), (3, HIGH))):
                put(
                    gbuf.at[at(j, x, h, far, part)],
                    r1.at[j, x, h, k],
                    send_s.at[j, x, h, k],
                    recv_s.at[j, x, h, k],
                    devs[h][0](d),
                )

    def g1(j, x):
        for h in range(2):
            i1 = index[h][0]
            for k, (d, low) in enumerate(((1, 0), (3, 2))):
                got(r1.at[j, x, h, k], recv_s.at[j, x, h, k])
                to = (i1 + d) % 4
                for a in range(2):
                    spot = at(j, x, h, to, low + a)
                    gbuf[spot] = (gbuf[spot].astype(F32) + r1[j, x, h, k, a].astype(F32)).astype(BF16)
                put(
                    gbuf.at[at(j, x, h, to)],
                    r2.at[j, x, h, k],
                    send_s.at[j, x, h, 2 + k],
                    recv_s.at[j, x, h, 2 + k],
                    devs[h][0](d),
                )

    def g2(j, x):
        for h in range(2):
            i1, i2 = index[h]
            for k in range(2):
                got(r2.at[j, x, h, k], recv_s.at[j, x, h, 2 + k])
            for d in (2, 1, 3, 0):
                a2 = (i2 + d) % 4
                spot = at(j, x, h, i1, a2)
                gbuf[spot] = (
                    gbuf[spot].astype(F32) + r2[j, x, h, 0, a2].astype(F32) + r2[j, x, h, 1, a2].astype(F32)
                ).astype(BF16)
                if d:
                    put(
                        gbuf.at[spot],
                        r3.at[j, x, h, d - 1],
                        send_s.at[j, x, h, 3 + d],
                        recv_s.at[j, x, h, 3 + d],
                        devs[h][1](d),
                    )

    def g3(j, x):
        for h in range(2):
            i1, i2 = index[h]
            for d in range(1, 4):
                got(r3.at[j, x, h, d - 1], recv_s.at[j, x, h, 3 + d])
            spot = at(j, x, h, i1, i2)
            total = gbuf[spot].astype(F32)
            for d in range(3):
                total = total + r3[j, x, h, d].astype(F32)
            gbuf[spot] = total.astype(BF16)

    def gx(j):
        for h in range(2):
            put(gbuf.at[at(j, 1 - xl, h, *index[h])], r4.at[j, h], send_s.at[j, 0, h, 14], recv_s.at[j, 0, h, 14], xdev)

    def gy(j):
        for k in range(3):
            loads[k * NJ + j].wait()
        inverse = jnp.broadcast_to(1.0 / count_out[0:1, 0:1], (32, FEAT))
        halves = []
        for h in range(2):
            got(r4.at[j, h], recv_s.at[j, 0, h, 14])
            halves.append(gbuf[at(j, xl, h, *index[h])].astype(F32) + r4[j, h].astype(F32))
        summed = jnp.concatenate(halves, axis=1).astype(BF16)
        g_out[j, y] = summed
        grad = summed.astype(F32) * inverse
        new, _, _ = adamw(*(mbuf[k, j].reshape(32, FEAT) for k in range(3)), grad)
        new = new.astype(BF16)
        for h in range(2):
            spot = at(j, xl, h, *index[h])
            wbuf[spot] = new[:, h * HALF : (h + 1) * HALF]
            own = wbuf.at[spot]
            put(own, own, send_s.at[j, 0, h, 15], recv_s.at[j, 0, h, 15], xdev)
        wa(j, 0)

    def gg(j):
        for d in range(1, 4):
            put(g_out.at[j, y], g_out.at[j, y], gg_s.at[j, d - 1], gg_r.at[j, d - 1], ydev(d))

    def side(k):
        return 1 - xl if k else xl

    def wa(j, k):
        for h in range(2):
            own = wbuf.at[at(j, side(k), h, *index[h])]
            if k:
                got(own, recv_s.at[j, 0, h, 15])
            for d in (2, 1, 3):
                put(own, own, send_s.at[j, k, h, 6 + d], recv_s.at[j, k, h, 6 + d], devs[h][1](d))

    def wb(j, k):
        for h in range(2):
            i1, i2 = index[h]
            for d in range(1, 4):
                got(wbuf.at[at(j, side(k), h, i1, (i2 + 4 - d) % 4)], recv_s.at[j, k, h, 6 + d])
            own = wbuf.at[at(j, side(k), h, i1)]
            for n, d in enumerate((1, 3)):
                put(own, own, send_s.at[j, k, h, 10 + n], recv_s.at[j, k, h, 10 + n], devs[h][0](d))

    def wc(j, k):
        for h in range(2):
            i1 = index[h][0]
            for n, (d, part) in enumerate(((1, LOW), (3, HIGH))):
                back = (i1 + 4 - d) % 4
                got(wbuf.at[at(j, side(k), h, back)], recv_s.at[j, k, h, 10 + n])
                piece = wbuf.at[at(j, side(k), h, back, part)]
                put(piece, piece, send_s.at[j, k, h, 12 + n], recv_s.at[j, k, h, 12 + n], devs[h][0](d))

    def wd(j, k):
        for h in range(2):
            far = (index[h][0] + 2) % 4
            for n, part in enumerate((LOW, HIGH)):
                got(wbuf.at[at(j, side(k), h, far, part)], recv_s.at[j, k, h, 12 + n])

        def times(rows, h):
            return jnp.dot(
                hbuf[j, side(k), rows], wbuf[j, side(k), h].reshape(512, HALF), preferred_element_type=F32
            )

        if (j, k) != (NJ - 1, 1):

            @pl.loop(0, 4)
            def _(b):
                rows = pl.ds(pl.multiple_of(b * 256, 256), 256)
                for h in range(2):
                    cols = slice(h * HALF, (h + 1) * HALF)
                    if (j, k) == (0, 0):
                        acc[rows, cols] = times(rows, h)
                    else:
                        acc[rows, cols] += times(rows, h)
        else:
            for b in range(4):
                core = 1 - c if b < 2 else c
                rows = pl.ds(pl.multiple_of(core * 512 + (b % 2) * 256, 256), 256)
                for h in range(2):
                    cols = slice(h * HALF, (h + 1) * HALF)
                    part = acc[rows, cols] + times(rows, h)
                    if b < 2:
                        fsend[b, :, cols] = part.astype(BF16)
                    else:
                        acc[rows, cols] = part
                if b < 2:
                    put(fsend.at[b], frecv.at[b], small_s.at[12 + b], small_r.at[12 + b], sib)

    def last():
        for b in range(2):
            got(frecv.at[b], small_r.at[12 + b])
            rows = pl.ds(pl.multiple_of(c * 512 + b * 256, 256), 256)
            fresh_out[b * 256 : (b + 1) * 256] = (acc[rows] + frecv[b].astype(F32)).astype(BF16)

    def count_stage(n):
        if n == 0:
            cnt[4 + z] = count_sum(0, 4, y, 0)
            count_step(4, 4, z, zdev, 4)
        elif n == 1:
            cnt[8 + xl] = count_sum(4, 4, z, 4)
            count_step(8, 2, xl, lambda d: xdev, 8)
        elif n == 2:
            cnt[10 + c] = count_sum(8, 2, xl, 8)
            count_step(10, 2, c, lambda d: sib, 10)
        else:
            count_out[...] = count_sum(10, 2, c, 10)

    for stage, j, x in schedule():
        if stage == "g0":
            g0(j, x)
        elif stage == "g1":
            g1(j, x)
        elif stage == "g2":
            g2(j, x)
        elif stage == "g3":
            g3(j, x)
        elif stage == "gx":
            gx(j)
        elif stage == "gy":
            gy(j)
        elif stage == "gg":
            gg(j)
        elif stage == "wa":
            wa(j, x)
        elif stage == "wb":
            wb(j, x)
        elif stage == "wc":
            wc(j, x)
        elif stage == "wd":
            wd(j, x)
        elif stage == "h":
            h_send(j)
        elif stage == "count":
            count_stage(x)
        else:
            last()

    for j in range(NJ):
        for d in range(1, 4):
            got(g_out.at[j, (y + 4 - d) % 4], gg_r.at[j, d - 1])
        for x in range(2):
            for k in range(3):
                whole = hbuf.at[j, x, mine]
                pltpu.make_async_remote_copy(
                    whole, whole, h_s.at[j, x, k], h_s.at[j, x, k], device_id=sib, device_id_type=MESH
                ).wait_send()
    for copy in sends:
        copy.wait_send()


def finish_kernel(g, count, master, first, second, fresh, new_master, new_first, new_second, fresh_out):
    rows = master.shape[0]
    summed = g[...].astype(F32).reshape(rows, 8, 128)
    grad = summed * jnp.broadcast_to((1.0 / count[...])[0:1, 0:1].reshape(1, 1, 1), (rows, 8, 128))
    a, b, d = adamw(master[...], first[...], second[...], grad)
    new_master[...] = a
    new_first[...] = b
    new_second[...] = d
    fresh_out[...] = fresh[...].astype(F32).reshape(rows, 8, 128).astype(BF16)


def tiles(array):
    n = array.shape[0]
    return array.reshape(n, 2, 4, 128).transpose(0, 2, 1, 3).reshape(n, 8, 128)


def untiles(array):
    n = array.shape[0]
    return array.reshape(n, 4, 2, 128).transpose(0, 2, 1, 3).reshape(n, 2, 512)


def local(hidden_in, lengths, kv_grad_out, master, moment_one, moment_two):
    kv = tiles(kv_grad_out)
    states = [tiles(a) for a in (master, moment_one, moment_two)]
    hbm = pl.BlockSpec(memory_space=pl.ANY)
    vmem = pl.BlockSpec(memory_space=pltpu.VMEM)
    dma = pltpu.SemaphoreType.DMA
    fresh, g, count = pl.pallas_call(
        main_kernel,
        out_shape=(
            jax.ShapeDtypeStruct((TOK, FEAT), BF16),
            jax.ShapeDtypeStruct((NJ, 4, 32, FEAT), BF16),
            jax.ShapeDtypeStruct((8, 128), F32),
        ),
        in_specs=[hbm, pl.BlockSpec(memory_space=pltpu.SMEM), pl.BlockSpec(memory_space=pltpu.HBM), hbm, hbm, hbm],
        out_specs=(vmem, vmem, vmem),
        scratch_shapes=[
            pltpu.VMEM((NJ, 2, 1024, 512), BF16),
            pltpu.VMEM((1024, FEAT), BF16),
            pltpu.VMEM((TOK, 8, 128), BF16),
            pltpu.VMEM((NJ, 2, 2, 4, 4, 32, HALF), BF16),
            pltpu.VMEM((NJ, 2, 2, 2, 2, 32, HALF), BF16),
            pltpu.VMEM((NJ, 2, 2, 2, 4, 32, HALF), BF16),
            pltpu.VMEM((NJ, 2, 2, 3, 32, HALF), BF16),
            pltpu.VMEM((NJ, 2, 32, HALF), BF16),
            pltpu.VMEM((NJ, 2, 2, 4, 4, 32, HALF), BF16),
            pltpu.VMEM((1024, FEAT), F32),
            pltpu.VMEM((2, 256, FEAT), BF16),
            pltpu.VMEM((2, 256, FEAT), BF16),
            pltpu.VMEM((3, NJ, 32, 8, 128), F32),
            pltpu.VMEM((12, 8, 128), F32),
            dma((NJ, 2, 2, 16)),
            dma((NJ, 2, 2, 16)),
            dma((NJ, 3)),
            dma((NJ, 3)),
            dma((NJ, 2, 3)),
            dma((NJ, 2, 4)),
            dma((NJ, 2)),
            dma((14,)),
            dma((14,)),
            dma((4 + 3 * NJ,)),
        ],
        compiler_params=pltpu.CompilerParams(
            collective_id=0, has_side_effects=True, vmem_limit_bytes=50 * 2**20
        ),
        name="project",
    )(hidden_in, lengths, kv, *states)
    g = g.reshape(TOK, FEAT)
    step = 64
    flat = pl.BlockSpec((step, FEAT), lambda i: (i, 0))
    cube = pl.BlockSpec((step, 8, 128), lambda i: (i, 0, 0))
    outs = pl.pallas_call(
        finish_kernel,
        grid=(TOK // step,),
        out_shape=[jax.ShapeDtypeStruct((TOK, 8, 128), F32)] * 3
        + [jax.ShapeDtypeStruct((TOK, 8, 128), BF16)],
        in_specs=[flat, pl.BlockSpec((8, 128), lambda i: (0, 0)), cube, cube, cube, flat],
        out_specs=[cube] * 4,
        compiler_params=pltpu.CompilerParams(vmem_limit_bytes=24 * 2**20),
        name="update",
    )(g, count, *states, fresh)
    return tuple(untiles(a) for a in outs)


def solution(mesh):
    in_specs = (
        P(("rep", "shard", "tp"), None),
        P(("rep", "shard")),
        P(("rep", "shard"), None, "tp"),
        P("shard", None, "tp"),
        P("shard", None, "tp"),
        P("shard", None, "tp"),
    )
    out_specs = (
        P("shard", None, "tp"),
        P("shard", None, "tp"),
        P("shard", None, "tp"),
        P(("rep", "shard"), None, "tp"),
    )
    return jax.shard_map(local, mesh=mesh, in_specs=in_specs, out_specs=out_specs, check_vma=False)
```
